32 devices in a mesh: var: 8 (over y, x, core), seq: 4 (over z).
Axes of the slice: x: 2, y: 2, z: 4, core: 2. Of those that a mesh axis runs over, the one named last changes fastest.
Arguments:
- patches: bfloat16 [48, 512, 64], P('var', 'seq'), may hold values from -6 to 6
- patch_weight: bfloat16 [48, 64, 4096], P('var'), may hold values from -0.75 to 0.75
- var_embed: bfloat16 [48, 4096], P('var'), may hold values from -1.71 to 4.5
- agg_query: bfloat16 [4096, 32], replicated, may hold values from -1.5 to 1000
- norm_gain: bfloat16 [4096], replicated, may hold values from 0.5 to 1.5
- qkv_weight: bfloat16 [4096, 3, 4096], P(None, None, 'var'), may hold values from -0.21875 to 0.21875
- out_weight: bfloat16 [4096, 4096], P('var'), may hold values from -0.09375 to 0.09375
- head_cot: bfloat16 [512, 3072], P('seq', 'var'), may hold values from -0.25 to 0.25
Outputs:
- head_grad: float32 [4096, 3072], P('seq', 'var')
The draws below stay inside these ranges and needn't reach their ends.
All inputs are finite; a program needn't handle non-finite values.
Results may differ from the reference program's by a relative error of at most 0.033.
The reference program's roundings to bfloat16 on the way count: a program that leaves them out, or rounds other values in their place, can miss the bound.
Values may be sent and summed in bfloat16 or wider, within the bound.
A program may use at most 128 MiB of HBM per device.

```python
import math
import jax
import jax.numpy as jnp
from jax import lax

D = 4096
HEADS = 32
HD = 128
P_SIZE = 64
V = 48
C = 3072
TOK_DEV = 128
TOKENS = 512


def draw_var_embed(key, part):
    key = jax.random.fold_in(key, 13)
    base = jax.random.uniform(key, (V, D), jnp.float32, -1.7, 1.7)
    return base.astype(jnp.bfloat16)


def draw_agg_query(key, part):
    key = jax.random.fold_in(key, 11)
    return jnp.clip(0.25 * jax.random.normal(key, (D, HEADS), jnp.float32), -1.5, 1.5).astype(jnp.bfloat16)


def draw_qkv_weight(key, part):
    key = jax.random.fold_in(key, 17)
    factor = D ** (-0.5)
    base = jnp.clip(jax.random.normal(key, (D, 3, D), jnp.float32), -4.0, 4.0) * factor
    return jnp.stack([3.0 * base[:, 0, :], base[:, 1, :], base[:, 2, :]], axis=1).astype(jnp.bfloat16)


def level_of(stream_key, dims, split, low, top_value):
    level, own = 1.0, jax.random.fold_in(stream_key, 6)
    for axis_at, blocks in split:
        heights = jnp.exp(jax.random.uniform(jax.random.fold_in(own, axis_at), (blocks,), jnp.float32, low / len(split), top_value / len(split)))
        level = level * jnp.repeat(heights, dims[axis_at] // blocks).reshape([-1 if axis == axis_at else 1 for axis in range(len(dims))])
    return level


def normal_values(stream_key, extent, scale, reach, split=(), kind=jnp.bfloat16):
    factor_of = level_of(stream_key, extent, split, -0.22, 0.18) if split else 1.0
    array = jax.random.normal(stream_key, extent, jnp.float32) * scale * factor_of
    return jnp.minimum(jnp.maximum(array, -reach), reach).astype(kind)


def setup_inputs(seed: int = 0) -> dict:
    seeds = jax.random.split(jax.random.key(seed), 9)
    patches = normal_values(seeds[0], (V, TOKENS, P_SIZE), 1.0, 6.0, ((0, 8), (1, 4)))
    patch_weight = normal_values(seeds[1], (V, P_SIZE, D), P_SIZE ** -0.5, 0.75, ((0, 8),))
    var_embed = draw_var_embed(jax.random.fold_in(seeds[8], 71), 0)
    agg_query = draw_agg_query(jax.random.fold_in(seeds[8], 71), 0)
    norm_gain = jnp.clip(1.0 + 0.1 * jax.random.normal(seeds[4], (D,), jnp.float32), 0.5, 1.5).astype(jnp.bfloat16)
    qkv_weight = draw_qkv_weight(jax.random.fold_in(seeds[8], 71), 0)
    out_weight = normal_values(seeds[6], (D, D), D ** -0.5, 0.09375, ((0, 8),))
    head_cot = normal_values(seeds[7], (TOKENS, C), TOKENS ** -0.5, 0.25, ((0, 4), (1, 8)))
    return dict(patches=patches, patch_weight=patch_weight, var_embed=var_embed, agg_query=agg_query, norm_gain=norm_gain, qkv_weight=qkv_weight, out_weight=out_weight, head_cot=head_cot)


eps = 1e-05

def aggregate_block(patch_block, patch_weight, var_embed, agg_query):
    embedded = jnp.einsum('vrp,vpd->vrd', patch_block.astype(jnp.float32), patch_weight.astype(jnp.float32))
    embedded = (embedded + var_embed.astype(jnp.float32)[:, None, :]).astype(jnp.bfloat16)
    count, rows, width = embedded.shape
    scores = jnp.dot(embedded.reshape(count * rows, width), agg_query, preferred_element_type=jnp.float32)
    scores = scores.reshape(count, rows, HEADS) / math.sqrt(HD)
    peak = lax.optimization_barrier(jnp.max(scores, axis=0))
    weights = jnp.exp(scores - peak[None])
    total = lax.optimization_barrier(jnp.sum(weights, axis=0))
    values = embedded.reshape(count, rows, HEADS, HD).astype(jnp.float32)
    numer = lax.optimization_barrier(jnp.sum(weights[..., None] * values, axis=0))
    return (numer / total[..., None]).reshape(rows, width).astype(jnp.bfloat16)

def layer_norm(tokens, gain):
    values = tokens.astype(jnp.float32)
    center = lax.optimization_barrier(jnp.mean(values, axis=-1, keepdims=True))
    shifted = values - center
    spread = lax.optimization_barrier(jnp.mean(shifted * shifted, axis=-1, keepdims=True))
    return (shifted * lax.rsqrt(spread + eps) * gain.astype(jnp.float32)).astype(jnp.bfloat16)

def attend_head(operands):
    query, keys, values = operands
    scores = jnp.dot(query, keys.T, preferred_element_type=jnp.float32) / math.sqrt(HD)
    peak = lax.optimization_barrier(jnp.max(scores, axis=-1, keepdims=True))
    weights = jnp.exp(scores - peak)
    total = lax.optimization_barrier(jnp.sum(weights, axis=-1, keepdims=True))
    mixed = jnp.dot(weights.astype(jnp.bfloat16), values, preferred_element_type=jnp.float32)
    return (mixed / total).astype(jnp.bfloat16)

def reference(patches, patch_weight, var_embed, agg_query, norm_gain, qkv_weight, out_weight, head_cot):
    blocks = TOKENS // TOK_DEV
    grouped = patches.reshape(V, blocks, TOK_DEV, P_SIZE).transpose(1, 0, 2, 3)
    aggregated = lax.map(lambda block: aggregate_block(block, patch_weight, var_embed, agg_query), grouped)
    aggregated = aggregated.reshape(TOKENS, D)
    normed = layer_norm(aggregated, norm_gain)
    qkv = jnp.dot(normed, qkv_weight.reshape(D, 3 * D), preferred_element_type=jnp.float32).astype(jnp.bfloat16)
    qkv = qkv.reshape(TOKENS, 3, HEADS, HD).transpose(1, 2, 0, 3)
    attended = lax.map(attend_head, (qkv[0], qkv[1], qkv[2]))
    attended = attended.transpose(1, 0, 2).reshape(TOKENS, D)
    projected = jnp.dot(attended, out_weight, preferred_element_type=jnp.float32)
    layer = (aggregated.astype(jnp.float32) + projected).astype(jnp.bfloat16)
    return lax.dot_general(layer, head_cot, (((0,), (0,)), ((), ())), preferred_element_type=jnp.float32)
```

```python
import functools
import math

import jax
import jax.numpy as jnp
from jax import lax
from jax.experimental import pallas as pl
from jax.experimental.pallas import tpu as pltpu
from jax.sharding import PartitionSpec as P

MESH = pl.DeviceIdType.MESH
F32 = jnp.float32
BF16 = jnp.bfloat16
eps = 1e-05
HD = 128


def dot(a, b, contract=((1,), (0,))):
    return lax.dot_general(a, b, (contract, ((), ())), preferred_element_type=F32)


def kernel(
    nv, ns,
    patches, pw_hbm, var_embed, query_map, gain, wqkv_hbm, wo_hbm, cot,
    gathered, cot_all,
    pw, wqkv, wo, emb, stats_own, stats_in, numer, factor, pair_in, pair_sum, chip_in,
    agg, normed, keys_own, values_own, keys_in, values_in, query, attended,
    part, pair_in2, pair_sum2, chip_in2, layer,
    local_sem, cot_send, cot_recv, stats_send, stats_recv, pair_send, pair_recv, chip_send, chip_recv,
    norm_send, norm_recv, norm_fsend, norm_frecv, key_send, key_recv, value_send, value_recv,
    pair2_send, pair2_recv, chip2_send, chip2_recv, layer_send, layer_recv,
    last_send, last_recv, last_fsend, last_frecv,
):
    count, _, rows = patches.shape
    width = pw.shape[2]
    heads = width // HD
    nch = nv // 2
    share = rows // nv
    cols = wo.shape[0]
    piece = width // ns
    me = lax.axis_index("var")
    band = lax.axis_index("seq")
    chip = me // 2
    core = me % 2
    mate = chip * 2 + (1 - core)
    order = list(range(1, nch)) + [0]
    pending = []

    def chip_at(k):
        return (chip + k) % nch

    def chip_from(k):
        return (chip + nch - k) % nch

    def send(src, dst, ssem, rsem, **target):
        copy = pltpu.make_async_remote_copy(
            src_ref=src, dst_ref=dst, send_sem=ssem, recv_sem=rsem, device_id=target, device_id_type=MESH
        )
        copy.start()
        pending.append(copy)
        return copy

    loads = [
        pltpu.make_async_copy(pw_hbm, pw, local_sem.at[0]),
        pltpu.make_async_copy(wqkv_hbm, wqkv, local_sem.at[1]),
        pltpu.make_async_copy(wo_hbm, wo, local_sem.at[2]),
    ]
    for load in loads:
        load.start()

    barrier = pltpu.get_barrier_semaphore()
    for k in range(1, nv):
        pl.semaphore_signal(barrier, inc=1, device_id={"var": (me + k) % nv}, device_id_type=MESH)
    for k in range(1, ns):
        pl.semaphore_signal(barrier, inc=1, device_id={"seq": (band + k) % ns}, device_id_type=MESH)

    loads[0].wait()
    tile = 512

    @pl.loop(0, width // tile)
    def _(t):
        at = pl.ds(pl.multiple_of(t * tile, tile), tile)
        for v in range(count):
            e = dot(patches[v], pw[v, :, at], ((0,), (0,)))
            emb[v, :, at] = (e + var_embed[v : v + 1, at].astype(F32)).astype(BF16)

    scores = [dot(query_map[...], emb[v], ((1,), (1,))) / math.sqrt(HD) for v in range(count)]
    peak = functools.reduce(jnp.maximum, scores)
    weights = [jnp.exp(s - peak) for s in scores]
    total = functools.reduce(jnp.add, weights)
    stats_own[0] = peak
    stats_own[1] = total

    pl.semaphore_wait(barrier, nv - 1 + ns - 1)
    stats = [
        send(stats_own, stats_in.at[k - 1], stats_send.at[k - 1], stats_recv.at[k - 1], var=(me + k) % nv)
        for k in range(1, nv)
    ]
    cots = [
        send(cot, cot_all.at[band], cot_send.at[k - 1], cot_recv.at[k - 1], seq=(band + k) % ns)
        for k in range(1, ns)
    ]
    cot_all[band] = cot[...]

    weights = [jnp.transpose(w) for w in weights]
    for h in range(heads):
        at = slice(h * HD, (h + 1) * HD)
        acc = weights[0][:, h : h + 1] * emb[0, :, at].astype(F32)
        for v in range(1, count):
            acc = acc + weights[v][:, h : h + 1] * emb[v, :, at].astype(F32)
        for d in range(nv):
            numer[d % 2, d // 2, :, at] = acc[d * share : (d + 1) * share]

    for copy in stats:
        copy.wait_recv()
    own_peak = stats_own[0]
    top = own_peak
    for k in range(nv - 1):
        top = jnp.maximum(top, stats_in[k, 0])
    whole = stats_own[1] * jnp.exp(own_peak - top)
    for k in range(nv - 1):
        whole = whole + stats_in[k, 1] * jnp.exp(stats_in[k, 0] - top)
    scale = jnp.transpose(jnp.exp(own_peak - top) / whole)
    for d in range(nv):
        factor[d % 2, d // 2] = scale[d * share : (d + 1) * share]

    def scaled(c, j, h):
        return numer[c, j, :, h * HD : (h + 1) * HD] * factor[c, j, :, h : h + 1]

    pairs = []
    for i, k in enumerate(order):
        j = chip_at(k)
        for h in range(heads):
            numer[1 - core, j, :, h * HD : (h + 1) * HD] = scaled(1 - core, j, h)
        pairs.append(
            send(numer.at[1 - core, j], pair_in.at[i], pair_send.at[i], pair_recv.at[i], var=mate)
        )
    chips = []
    for i, k in enumerate(order):
        j = chip_at(k)
        pairs[i].wait_recv()
        for h in range(heads):
            at = slice(h * HD, (h + 1) * HD)
            pair_sum[i, :, at] = scaled(core, j, h) + pair_in[i, :, at]
        if k:
            chips.append(
                send(pair_sum.at[i], chip_in.at[i], chip_send.at[i], chip_recv.at[i], var=2 * j + core)
            )
    for copy in chips:
        copy.wait_recv()
    sums = pair_sum[nch - 1]
    for i in range(nch - 1):
        sums = sums + chip_in[i]
    own = sums.astype(BF16)
    agg[...] = own

    own = own.astype(F32)
    center = jnp.mean(own, axis=-1, keepdims=True)
    shifted = own - center
    spread = jnp.mean(shifted * shifted, axis=-1, keepdims=True)
    normed[me] = (shifted * lax.rsqrt(spread + eps) * gain[...].astype(F32)).astype(BF16)

    def gather(part_of, ssem, rsem, fsend, frecv):
        mine = part_of(me)
        direct = [
            send(mine, mine, ssem.at[k - 1], rsem.at[k - 1], var=2 * chip_at(k) + core) for k in range(1, nch)
        ]
        across = [send(mine, mine, fsend.at[0], frecv.at[0], var=mate)]
        for k in range(1, nch):
            direct[k - 1].wait_recv()
            got = part_of(2 * chip_from(k) + core)
            across.append(send(got, got, fsend.at[k], frecv.at[k], var=mate))
        for copy in across:
            copy.wait_recv()

    gather(lambda d: normed.at[d], norm_send, norm_recv, norm_fsend, norm_frecv)

    step = 256
    loads[1].wait()

    def project(which, out):
        @pl.loop(0, cols // step)
        def _(t):
            at = pl.ds(pl.multiple_of(t * step, step), step)
            out[:, at] = dot(normed[...].reshape(rows, width), wqkv[which, :, at]).astype(BF16)

    project(1, keys_own)
    key_copies = [
        send(keys_own, keys_in.at[k - 1], key_send.at[k - 1], key_recv.at[k - 1], seq=(band + k) % ns)
        for k in range(1, ns)
    ]
    project(2, values_own)
    value_copies = [
        send(values_own, values_in.at[k - 1], value_send.at[k - 1], value_recv.at[k - 1], seq=(band + k) % ns)
        for k in range(1, ns)
    ]
    project(0, query)
    for copy in key_copies:
        copy.wait_recv()
    probs, totals = [], []
    for h in range(cols // HD):
        at = slice(h * HD, (h + 1) * HD)
        q = query[:, at]
        blocks = [dot(q, keys_own[:, at], ((1,), (1,)))]
        blocks += [dot(q, keys_in[k, :, at], ((1,), (1,))) for k in range(ns - 1)]
        s = jnp.concatenate(blocks, axis=1) / math.sqrt(HD)
        e = jnp.exp(s - jnp.max(s, axis=-1, keepdims=True))
        totals.append(jnp.sum(e, axis=-1, keepdims=True))
        probs.append(e.astype(BF16))
    for copy in value_copies:
        copy.wait_recv()
    for h in range(cols // HD):
        at = slice(h * HD, (h + 1) * HD)
        vals = jnp.concatenate([values_own[:, at]] + [values_in[k, :, at] for k in range(ns - 1)], axis=0)
        attended[:, at] = (dot(probs[h], vals) / totals[h]).astype(BF16)

    loads[2].wait()

    @pl.loop(0, width // tile)
    def _(t):
        at = pl.ds(pl.multiple_of(t * tile, tile), tile)
        p = dot(attended[...], wo[:, at])
        for d in range(nv):
            part[d % 2, d // 2, :, at] = p[d * share : (d + 1) * share]

    pairs = [
        send(part.at[1 - core, chip_at(k)], pair_in2.at[i], pair2_send.at[i], pair2_recv.at[i], var=mate)
        for i, k in enumerate(order)
    ]
    chips = []
    for i, k in enumerate(order):
        j = chip_at(k)
        pairs[i].wait_recv()
        if k:
            pair_sum2[i] = (part[core, j] + pair_in2[i]).astype(BF16)
            chips.append(
                send(pair_sum2.at[i], chip_in2.at[i], chip2_send.at[i], chip2_recv.at[i], var=2 * j + core)
            )
    sums = agg[...].astype(F32) + (part[core, chip] + pair_in2[nch - 1])
    for i in range(nch - 1):
        chips[i].wait_recv()
        sums = sums + chip_in2[i].astype(F32)
    sums = sums.astype(BF16)
    for s in range(ns):
        layer[s] = sums[:, s * piece : (s + 1) * piece]

    copies = [
        send(
            layer.at[(band + k) % ns], gathered.at[band, me], layer_send.at[k - 1], layer_recv.at[k - 1],
            seq=(band + k) % ns,
        )
        for k in range(1, ns)
    ]
    gathered[band, me] = layer[band]
    for copy in copies:
        copy.wait_recv()
    gather(lambda d: gathered.at[:, d], last_send, last_recv, last_fsend, last_frecv)
    for copy in cots:
        copy.wait_recv()
    for copy in pending:
        copy.wait_send()


def body(nv, ns, patches, patch_weight, var_embed, agg_query, norm_gain, qkv_weight, out_weight, head_cot):
    count, rows, pixels = patches.shape
    width = patch_weight.shape[2]
    heads = agg_query.shape[1]
    cols = out_weight.shape[0]
    share = rows // nv
    nch = nv // 2
    piece = width // ns
    dma = pltpu.SemaphoreType.DMA
    vmem = pl.BlockSpec(memory_space=pltpu.VMEM)
    anywhere = pl.BlockSpec(memory_space=pl.ANY)
    V = pltpu.VMEM
    gathered, cot_all = pl.pallas_call(
        functools.partial(kernel, nv, ns),
        out_shape=[
            jax.ShapeDtypeStruct((ns, nv, share, piece), BF16),
            jax.ShapeDtypeStruct((ns,) + head_cot.shape, BF16),
        ],
        in_specs=[vmem, anywhere, vmem, vmem, vmem, anywhere, anywhere, vmem],
        out_specs=[vmem, vmem],
        scratch_shapes=[
            V((count, pixels, width), BF16),
            V((3, width, cols), BF16),
            V((cols, width), BF16),
            V((count, rows, width), BF16),
            V((2, heads, rows), F32),
            V((nv - 1, 2, heads, rows), F32),
            V((2, nch, share, width), F32),
            V((2, nch, share, heads), F32),
            V((nch, share, width), F32),
            V((nch, share, width), F32),
            V((nch - 1, share, width), F32),
            V((share, width), BF16),
            V((nv, share, width), BF16),
            V((rows, cols), BF16),
            V((rows, cols), BF16),
            V((ns - 1, rows, cols), BF16),
            V((ns - 1, rows, cols), BF16),
            V((rows, cols), BF16),
            V((rows, cols), BF16),
            V((2, nch, share, width), F32),
            V((nch, share, width), F32),
            V((nch - 1, share, width), BF16),
            V((nch - 1, share, width), BF16),
            V((ns, share, piece), BF16),
            dma((3,)),
            dma((ns - 1,)), dma((ns - 1,)),
            dma((nv - 1,)), dma((nv - 1,)),
            dma((nch,)), dma((nch,)),
            dma((nch - 1,)), dma((nch - 1,)),
            dma((nch - 1,)), dma((nch - 1,)), dma((nch,)), dma((nch,)),
            dma((ns - 1,)), dma((ns - 1,)), dma((ns - 1,)), dma((ns - 1,)),
            dma((nch,)), dma((nch,)),
            dma((nch - 1,)), dma((nch - 1,)),
            dma((ns - 1,)), dma((ns - 1,)),
            dma((nch - 1,)), dma((nch - 1,)), dma((nch,)), dma((nch,)),
        ],
        compiler_params=pltpu.CompilerParams(
            collective_id=0, has_side_effects=True, vmem_limit_bytes=56 * 1024 * 1024
        ),
    )(
        jnp.transpose(patches, (0, 2, 1)),
        patch_weight,
        var_embed,
        jnp.transpose(agg_query),
        norm_gain.reshape(1, width),
        jnp.transpose(qkv_weight, (1, 0, 2)),
        out_weight,
        head_cot,
    )
    tokens = ns * rows
    return lax.dot_general(
        gathered.reshape(tokens, piece),
        cot_all.reshape(tokens, head_cot.shape[1]),
        (((0,), (0,)), ((), ())),
        preferred_element_type=F32,
    )


def solution(mesh):
    nv, ns = mesh.shape["var"], mesh.shape["seq"]
    return jax.shard_map(
        functools.partial(body, nv, ns),
        mesh=mesh,
        in_specs=(
            P("var", "seq", None),
            P("var", None, None),
            P("var", None),
            P(),
            P(),
            P(None, None, "var"),
            P("var", None),
            P("seq", "var"),
        ),
        out_specs=P("seq", "var"),
        check_vma=False,
    )
```

```python
import functools
import math

import jax
import jax.numpy as jnp
from jax import lax
from jax.experimental import pallas as pl
from jax.experimental.pallas import tpu as pltpu
from jax.sharding import PartitionSpec as P

MESH = pl.DeviceIdType.MESH
F32 = jnp.float32
BF16 = jnp.bfloat16
eps = 1e-05
HD = 128


def dot(a, b, contract=((1,), (0,))):
    return lax.dot_general(a, b, (contract, ((), ())), preferred_element_type=F32)


def kernel(
    nv, ns,
    patches, pw_hbm, var_embed, query_map, gain, wqkv_hbm, wo_hbm, cot,
    gathered, cot_all,
    pw, wqkv, wo, emb, weights, stats_own, stats_in, for_mate, factor, pair_in, pair_sum, chip_in,
    agg, normed, keys_own, values_own, query_own, keys_in, values_in, query_in, mixed, attended,
    part, pair_in2, pair_sum2, chip_in2, layer,
    pw_sem, local_sem, cot_send, cot_recv, stats_send, stats_recv, pair_send, pair_recv, chip_send, chip_recv,
    norm_send, norm_recv, norm_fsend, norm_frecv, key_send, key_recv, value_send, value_recv,
    query_send, query_recv, mixed_send, mixed_recv,
    pair2_send, pair2_recv, chip2_send, chip2_recv, layer_send, layer_recv,
    last_send, last_recv, last_fsend, last_frecv,
):
    count, _, rows = patches.shape
    width = pw.shape[2]
    heads = width // HD
    nch = nv // 2
    share = rows // nv
    cols = wo.shape[0]
    piece = width // ns
    spread_heads = cols // HD % ns == 0
    groups, _, gcols = attended.shape
    me = lax.axis_index("var")
    band = lax.axis_index("seq")
    chip = me // 2
    core = me % 2
    mate = chip * 2 + (1 - core)
    order = list(range(1, nch)) + [0]
    pending = []

    def chip_at(k):
        return (chip + k) % nch

    def chip_from(k):
        return (chip + nch - k) % nch

    def send(src, dst, ssem, rsem, **target):
        copy = pltpu.make_async_remote_copy(
            src_ref=src, dst_ref=dst, send_sem=ssem, recv_sem=rsem, device_id=target, device_id_type=MESH
        )
        copy.start()
        pending.append(copy)
        return copy

    embed_loads = [pltpu.make_async_copy(pw_hbm.at[v], pw.at[v], pw_sem.at[v]) for v in range(count)]
    for load in embed_loads:
        load.start()
    loads = [
        pltpu.make_async_copy(wqkv_hbm, wqkv, local_sem.at[0]),
        pltpu.make_async_copy(wo_hbm, wo, local_sem.at[1]),
    ]

    barrier = pltpu.get_barrier_semaphore()
    for k in range(1, nv):
        pl.semaphore_signal(barrier, inc=1, device_id={"var": (me + k) % nv}, device_id_type=MESH)
    for k in range(1, ns):
        pl.semaphore_signal(barrier, inc=1, device_id={"seq": (band + k) % ns}, device_id_type=MESH)

    tile = 512
    scores = []
    for v in range(count):
        embed_loads[v].wait()
        if v == count - 1:
            for load in loads:
                load.start()
        pixels = jnp.transpose(patches[v])

        @pl.loop(0, width // tile)
        def _(t):
            at = pl.ds(pl.multiple_of(t * tile, tile), tile)
            e = (dot(pixels, pw[v, :, at]) + var_embed[v : v + 1, at].astype(F32)).astype(BF16)
            for d in range(nv):
                emb[v, d, :, at] = e[d * share : (d + 1) * share]

        scores.append(dot(query_map[...], emb[v].reshape(rows, width), ((1,), (1,))) / math.sqrt(HD))
    peak = functools.reduce(jnp.maximum, scores)
    unscaled = [jnp.exp(s - peak) for s in scores]
    total = functools.reduce(jnp.add, unscaled)
    stats_own[0] = peak
    stats_own[1] = total

    pl.semaphore_wait(barrier, nv - 1 + ns - 1)
    stats = [
        send(stats_own, stats_in.at[k - 1], stats_send.at[k - 1], stats_recv.at[k - 1], var=(me + k) % nv)
        for k in range(1, nv)
    ]
    cots = [
        send(cot, cot_all.at[band], cot_send.at[k - 1], cot_recv.at[k - 1], seq=(band + k) % ns)
        for k in range(1, ns)
    ]
    cot_all[band] = cot[...]

    for v in range(count):
        w = jnp.transpose(unscaled[v])
        for d in range(nv):
            weights[v, d] = w[d * share : (d + 1) * share]

    def weighted(d):
        w = [weights[v, d] for v in range(count)]
        for h in range(heads):
            at = slice(h * HD, (h + 1) * HD)
            acc = w[0][:, h : h + 1] * emb[0, d, :, at].astype(F32)
            for v in range(1, count):
                acc = acc + w[v][:, h : h + 1] * emb[v, d, :, at].astype(F32)
            yield h, at, acc

    pairs = []
    for i, k in enumerate(order):
        for h, at, acc in weighted(2 * chip_at(k) + 1 - core):
            for_mate[i, :, at] = acc
        pairs.append(send(for_mate.at[i], pair_in.at[i], pair_send.at[i], pair_recv.at[i], var=mate))

    for copy in stats:
        copy.wait_recv()
    own_peak = stats_own[0]
    top = own_peak
    for k in range(nv - 1):
        top = jnp.maximum(top, stats_in[k, 0])
    whole = stats_own[1] * jnp.exp(own_peak - top)
    for k in range(nv - 1):
        whole = whole + stats_in[k, 1] * jnp.exp(stats_in[k, 0] - top)
    mate_peak = stats_in[(1 - core) * (nv - 2), 0]
    for which, part_peak in enumerate((own_peak, mate_peak)):
        scale = jnp.transpose(jnp.exp(part_peak - top) / whole)
        for d in range(nv):
            factor[which, d] = scale[d * share : (d + 1) * share]

    chips = []
    for i, k in enumerate(order):
        d = 2 * chip_at(k) + core
        own_factor, mate_factor = factor[0, d], factor[1, d]
        pairs[i].wait_recv()
        for h, at, acc in weighted(d):
            pair_sum[i, :, at] = acc * own_factor[:, h : h + 1] + pair_in[i, :, at] * mate_factor[:, h : h + 1]
        if k:
            chips.append(send(pair_sum.at[i], chip_in.at[i], chip_send.at[i], chip_recv.at[i], var=d))
    for copy in chips:
        copy.wait_recv()
    sums = pair_sum[nch - 1]
    for i in range(nch - 1):
        sums = sums + chip_in[i]
    own = sums.astype(BF16)
    agg[...] = own

    own = own.astype(F32)
    center = jnp.mean(own, axis=-1, keepdims=True)
    shifted = own - center
    spread = jnp.mean(shifted * shifted, axis=-1, keepdims=True)
    normed[me] = (shifted * lax.rsqrt(spread + eps) * gain[...].astype(F32)[None, :]).astype(BF16)

    def gather(part_of, ssem, rsem, fsend, frecv):
        mine = part_of(me)
        direct = [
            send(mine, mine, ssem.at[k - 1], rsem.at[k - 1], var=2 * chip_at(k) + core) for k in range(1, nch)
        ]
        across = [send(mine, mine, fsend.at[0], frecv.at[0], var=mate)]
        for k in range(1, nch):
            direct[k - 1].wait_recv()
            got = part_of(2 * chip_from(k) + core)
            across.append(send(got, got, fsend.at[k], frecv.at[k], var=mate))
        for copy in across:
            copy.wait_recv()

    gather(lambda d: normed.at[d], norm_send, norm_recv, norm_fsend, norm_frecv)

    step = 256
    loads[0].wait()

    def plane(k):
        return (band + k) % ns if spread_heads else 0

    def project(which, out):
        for t in range(cols // step):
            p = dot(normed[...].reshape(rows, width), wqkv[which, :, t * step : (t + 1) * step]).astype(BF16)
            span = min(step, gcols)
            for c in range(0, step, span):
                at = t * step + c
                out[at // gcols, :, at % gcols : at % gcols + span] = p[:, c : c + span]

    def to_bands(own, landing, ssem, rsem):
        return [
            send(own.at[plane(k)], landing.at[k - 1], ssem.at[k - 1], rsem.at[k - 1], seq=(band + k) % ns)
            for k in range(1, ns)
        ]

    project(1, keys_own)
    copies = to_bands(keys_own, keys_in, key_send, key_recv)
    project(0, query_own)
    if spread_heads:
        copies += to_bands(query_own, query_in, query_send, query_recv)
    project(2, values_own)
    value_copies = to_bands(values_own, values_in, value_send, value_recv)
    for copy in copies:
        copy.wait_recv()

    def all_rows(own, landing, at):
        return jnp.concatenate([own[plane(0), :, at]] + [landing[k, :, at] for k in range(ns - 1)], axis=0)

    sources = list(range(1, ns)) + [0] if spread_heads else [0]
    ready = {}
    for h in range(gcols // HD):
        at = slice(h * HD, (h + 1) * HD)
        keys = all_rows(keys_own, keys_in, at)
        for k in sources:
            q = query_in[k - 1, :, at] if k else query_own[plane(0), :, at]
            s = dot(q, keys, ((1,), (1,))) / math.sqrt(HD)
            e = jnp.exp(s - jnp.max(s, axis=-1, keepdims=True))
            ready[h, k] = e.astype(BF16), jnp.sum(e, axis=-1, keepdims=True)
    for copy in value_copies:
        copy.wait_recv()
    copies = []
    for k in sources:
        for h in range(gcols // HD):
            at = slice(h * HD, (h + 1) * HD)
            probs, total = ready[h, k]
            out = (dot(probs, all_rows(values_own, values_in, at)) / total).astype(BF16)
            if k:
                mixed[k - 1, :, at] = out
            else:
                attended[plane(0), :, at] = out
        if k:
            copies.append(
                send(
                    mixed.at[k - 1], attended.at[band], mixed_send.at[k - 1], mixed_recv.at[k - 1],
                    seq=(band + ns - k) % ns,
                )
            )
    for copy in copies:
        copy.wait_recv()

    loads[1].wait()
    attended_all = jnp.concatenate([attended[g] for g in range(groups)], axis=1)

    @pl.loop(0, width // tile)
    def _(t):
        at = pl.ds(pl.multiple_of(t * tile, tile), tile)
        p = dot(attended_all, wo[:, at])
        for d in range(nv):
            part[d % 2, d // 2, :, at] = p[d * share : (d + 1) * share]

    pairs = [
        send(part.at[1 - core, chip_at(k)], pair_in2.at[i], pair2_send.at[i], pair2_recv.at[i], var=mate)
        for i, k in enumerate(order)
    ]
    chips = []
    for i, k in enumerate(order):
        j = chip_at(k)
        pairs[i].wait_recv()
        if k:
            pair_sum2[i] = (part[core, j] + pair_in2[i]).astype(BF16)
            chips.append(
                send(pair_sum2.at[i], chip_in2.at[i], chip2_send.at[i], chip2_recv.at[i], var=2 * j + core)
            )
    sums = agg[...].astype(F32) + (part[core, chip] + pair_in2[nch - 1])
    for i in range(nch - 1):
        chips[i].wait_recv()
        sums = sums + chip_in2[i].astype(F32)
    sums = sums.astype(BF16)
    for s in range(ns):
        layer[s] = sums[:, s * piece : (s + 1) * piece]

    copies = [
        send(
            layer.at[(band + k) % ns], gathered.at[band, me], layer_send.at[k - 1], layer_recv.at[k - 1],
            seq=(band + k) % ns,
        )
        for k in range(1, ns)
    ]
    gathered[band, me] = layer[band]
    for copy in copies:
        copy.wait_recv()
    gather(lambda d: gathered.at[:, d], last_send, last_recv, last_fsend, last_frecv)
    for copy in cots:
        copy.wait_recv()
    for copy in pending:
        copy.wait_send()


def body(nv, ns, patches, patch_weight, var_embed, agg_query, norm_gain, qkv_weight, out_weight, head_cot):
    count, rows, pixels = patches.shape
    width = patch_weight.shape[2]
    heads = agg_query.shape[1]
    cols = out_weight.shape[0]
    share = rows // nv
    nch = nv // 2
    piece = width // ns
    groups = ns if cols // HD % ns == 0 else 1
    plane = (groups, rows, cols // groups)
    landing = (ns - 1, rows, cols // groups)
    dma = pltpu.SemaphoreType.DMA
    vmem = pl.BlockSpec(memory_space=pltpu.VMEM)
    anywhere = pl.BlockSpec(memory_space=pl.ANY)
    V = pltpu.VMEM
    gathered, cot_all = pl.pallas_call(
        functools.partial(kernel, nv, ns),
        out_shape=[
            jax.ShapeDtypeStruct((ns, nv, share, piece), BF16),
            jax.ShapeDtypeStruct((ns,) + head_cot.shape, BF16),
        ],
        in_specs=[vmem, anywhere, vmem, vmem, vmem, anywhere, anywhere, vmem],
        out_specs=[vmem, vmem],
        scratch_shapes=[
            V((count, pixels, width), BF16),
            V((3, width, cols), BF16),
            V((cols, width), BF16),
            V((count, nv, share, width), BF16),
            V((count, nv, share, heads), F32),
            V((2, heads, rows), F32),
            V((nv - 1, 2, heads, rows), F32),
            V((nch, share, width), F32),
            V((2, nv, share, heads), F32),
            V((nch, share, width), F32),
            V((nch, share, width), F32),
            V((nch - 1, share, width), F32),
            V((share, width), BF16),
            V((nv, share, width), BF16),
            V(plane, BF16),
            V(plane, BF16),
            V(plane, BF16),
            V(landing, BF16),
            V(landing, BF16),
            V(landing, BF16),
            V(landing, BF16),
            V(plane, BF16),
            V((2, nch, share, width), F32),
            V((nch, share, width), F32),
            V((nch - 1, share, width), BF16),
            V((nch - 1, share, width), BF16),
            V((ns, share, piece), BF16),
            dma((count,)),
            dma((2,)),
            dma((ns - 1,)), dma((ns - 1,)),
            dma((nv - 1,)), dma((nv - 1,)),
            dma((nch,)), dma((nch,)),
            dma((nch - 1,)), dma((nch - 1,)),
            dma((nch - 1,)), dma((nch - 1,)), dma((nch,)), dma((nch,)),
            dma((ns - 1,)), dma((ns - 1,)), dma((ns - 1,)), dma((ns - 1,)),
            dma((ns - 1,)), dma((ns - 1,)), dma((ns - 1,)), dma((ns - 1,)),
            dma((nch,)), dma((nch,)),
            dma((nch - 1,)), dma((nch - 1,)),
            dma((ns - 1,)), dma((ns - 1,)),
            dma((nch - 1,)), dma((nch - 1,)), dma((nch,)), dma((nch,)),
        ],
        compiler_params=pltpu.CompilerParams(
            collective_id=0, has_side_effects=True, vmem_limit_bytes=56 * 1024 * 1024
        ),
    )(
        jnp.transpose(patches, (0, 2, 1)),
        patch_weight,
        var_embed,
        jnp.transpose(agg_query),
        norm_gain,
        jnp.transpose(qkv_weight, (1, 0, 2)),
        out_weight,
        head_cot,
    )
    tokens = ns * rows
    return lax.dot_general(
        gathered.reshape(tokens, piece),
        cot_all.reshape(tokens, head_cot.shape[1]),
        (((0,), (0,)), ((), ())),
        preferred_element_type=F32,
    )


def solution(mesh):
    nv, ns = mesh.shape["var"], mesh.shape["seq"]
    return jax.shard_map(
        functools.partial(body, nv, ns),
        mesh=mesh,
        in_specs=(
            P("var", "seq", None),
            P("var", None, None),
            P("var", None),
            P(),
            P(),
            P(None, None, "var"),
            P("var", None),
            P("seq", "var"),
        ),
        out_specs=P("seq", "var"),
        check_vma=False,
    )
```

```python
import functools
import math

import jax
import jax.numpy as jnp
from jax import lax
from jax.experimental import pallas as pl
from jax.experimental.pallas import tpu as pltpu
from jax.sharding import PartitionSpec as P

MESH = pl.DeviceIdType.MESH
F32 = jnp.float32
BF16 = jnp.bfloat16
eps = 1e-05
HD = 128


def dot(a, b, contract=((1,), (0,))):
    return lax.dot_general(a, b, (contract, ((), ())), preferred_element_type=F32)


def kernel(
    nv, ns,
    patches, pw_hbm, var_embed, query_map, gain, wqkv_hbm, wo_hbm, cot,
    gathered, cot_all,
    pw, wqkv, wo, emb, weights, stats_own, stats_in, for_mate, factor, pair_in, pair_sum, chip_in,
    agg, normed, keys_own, values_own, query_own, keys_in, values_in, query_in, mixed, attended, products,
    part, pair_in2, pair_sum2, chip_in2, layer,
    pw_sem, local_sem, cot_send, cot_recv, stats_send, stats_recv, pair_send, pair_recv, chip_send, chip_recv,
    norm_send, norm_recv, norm_fsend, norm_frecv, key_send, key_recv, value_send, value_recv,
    query_send, query_recv, mixed_send, mixed_recv,
    pair2_send, pair2_recv, chip2_send, chip2_recv, layer_send, layer_recv,
    last_send, last_recv, last_fsend, last_frecv,
):
    count, _, rows = patches.shape
    width = pw.shape[2]
    heads = width // HD
    nch = nv // 2
    share = rows // nv
    cols = wo.shape[0]
    piece = width // ns
    half = width // 2
    sub = piece // 2
    spread_heads = cols // HD % ns == 0
    groups, _, gcols = attended.shape
    me = lax.axis_index("var")
    band = lax.axis_index("seq")
    chip = me // 2
    core = me % 2
    mate = chip * 2 + (1 - core)
    order = list(range(1, nch)) + [0]
    pending = []

    def chip_at(k):
        return (chip + k) % nch

    def chip_from(k):
        return (chip + nch - k) % nch

    def send(src, dst, ssem, rsem, **target):
        copy = pltpu.make_async_remote_copy(
            src_ref=src, dst_ref=dst, send_sem=ssem, recv_sem=rsem, device_id=target, device_id_type=MESH
        )
        copy.start()
        pending.append(copy)
        return copy

    embed_loads = [pltpu.make_async_copy(pw_hbm.at[v], pw.at[v], pw_sem.at[v]) for v in range(count)]
    for load in embed_loads:
        load.start()
    loads = [
        pltpu.make_async_copy(wqkv_hbm, wqkv, local_sem.at[0]),
        pltpu.make_async_copy(wo_hbm, wo, local_sem.at[1]),
    ]

    barrier = pltpu.get_barrier_semaphore()
    for k in range(1, nv):
        pl.semaphore_signal(barrier, inc=1, device_id={"var": (me + k) % nv}, device_id_type=MESH)
    for k in range(1, ns):
        pl.semaphore_signal(barrier, inc=1, device_id={"seq": (band + k) % ns}, device_id_type=MESH)

    tile = 512
    scores = []
    for v in range(count):
        embed_loads[v].wait()
        if v == count - 1:
            for load in loads:
                load.start()
        pixels = jnp.transpose(patches[v])
        s = None
        for t in range(0, width, tile):
            at = slice(t, t + tile)
            e = (dot(pixels, pw[v, :, at]) + var_embed[v : v + 1, at].astype(F32)).astype(BF16)
            for d in range(nv):
                emb[v, d, :, at] = e[d * share : (d + 1) * share]
            p = dot(e, query_map[:, at], ((1,), (1,)))
            s = p if s is None else s + p
        scores.append(s / math.sqrt(HD))
    peak = functools.reduce(jnp.maximum, scores)
    unscaled = [jnp.exp(s - peak) for s in scores]
    total = functools.reduce(jnp.add, unscaled)
    stats_own[0] = jnp.transpose(peak)
    stats_own[1] = jnp.transpose(total)

    pl.semaphore_wait(barrier, nv - 1 + ns - 1)
    stats = [
        send(stats_own, stats_in.at[k - 1], stats_send.at[k - 1], stats_recv.at[k - 1], var=(me + k) % nv)
        for k in range(1, nv)
    ]
    cots = [
        send(cot, cot_all.at[band], cot_send.at[k - 1], cot_recv.at[k - 1], seq=(band + k) % ns)
        for k in range(1, ns)
    ]
    cot_all[band] = cot[...]

    for v in range(count):
        w = unscaled[v]
        for d in range(nv):
            weights[v, d] = w[d * share : (d + 1) * share]

    def weighted(d):
        w = [weights[v, d] for v in range(count)]
        for h in range(heads):
            at = slice(h * HD, (h + 1) * HD)
            acc = w[0][:, h : h + 1] * emb[0, d, :, at].astype(F32)
            for v in range(1, count):
                acc = acc + w[v][:, h : h + 1] * emb[v, d, :, at].astype(F32)
            yield h, at, acc

    pairs = []
    for i, k in enumerate(order):
        for h, at, acc in weighted(2 * chip_at(k) + 1 - core):
            for_mate[i, :, at] = acc
        pairs.append(send(for_mate.at[i], pair_in.at[i], pair_send.at[i], pair_recv.at[i], var=mate))

    for copy in stats:
        copy.wait_recv()
    own_peak = stats_own[0]
    top = own_peak
    for k in range(nv - 1):
        top = jnp.maximum(top, stats_in[k, 0])
    whole = stats_own[1] * jnp.exp(own_peak - top)
    for k in range(nv - 1):
        whole = whole + stats_in[k, 1] * jnp.exp(stats_in[k, 0] - top)
    mate_peak = stats_in[(1 - core) * (nv - 2), 0]
    for which, part_peak in enumerate((own_peak, mate_peak)):
        scale = jnp.transpose(jnp.exp(part_peak - top) / whole)
        for d in range(nv):
            factor[which, d] = scale[d * share : (d + 1) * share]

    chips = []
    for i, k in enumerate(order):
        d = 2 * chip_at(k) + core
        own_factor, mate_factor = factor[0, d], factor[1, d]
        pairs[i].wait_recv()
        for h, at, acc in weighted(d):
            pair_sum[i, :, at] = acc * own_factor[:, h : h + 1] + pair_in[i, :, at] * mate_factor[:, h : h + 1]
        if k:
            chips.append(send(pair_sum.at[i], chip_in.at[i], chip_send.at[i], chip_recv.at[i], var=d))
    for copy in chips:
        copy.wait_recv()
    sums = pair_sum[nch - 1]
    for i in range(nch - 1):
        sums = sums + chip_in[i]
    own = sums.astype(BF16)
    for a in range(2):
        for b in range(ns):
            agg[a, :, b * sub : (b + 1) * sub] = own[:, b * piece + a * sub : b * piece + (a + 1) * sub]

    own = own.astype(F32)
    center = jnp.mean(own, axis=-1, keepdims=True)
    shifted = own - center
    spread = jnp.mean(shifted * shifted, axis=-1, keepdims=True)
    own = (shifted * lax.rsqrt(spread + eps) * gain[...].astype(F32)[None, :]).astype(BF16)
    for a in range(2):
        normed[a, me] = own[:, a * half : (a + 1) * half]

    def gather_start(part_of, a, ssem, rsem, fsend, frecv):
        mine = part_of(me)
        at = a * (nch - 1) - 1
        direct = [
            send(mine, mine, ssem.at[at + k], rsem.at[at + k], var=2 * chip_at(k) + core) for k in range(1, nch)
        ]
        return direct, [send(mine, mine, fsend.at[a * nch], frecv.at[a * nch], var=mate)]

    def gather_forward(part_of, a, direct, across, fsend, frecv):
        for k in range(1, nch):
            direct[k - 1].wait_recv()
            got = part_of(2 * chip_from(k) + core)
            across.append(send(got, got, fsend.at[a * nch + k], frecv.at[a * nch + k], var=mate))

    def gather_end(across):
        for copy in across:
            copy.wait_recv()

    norm_parts = [lambda d, a=a: normed.at[a, d] for a in range(2)]
    started = [
        gather_start(norm_parts[a], a, norm_send, norm_recv, norm_fsend, norm_frecv) for a in range(2)
    ]

    step = 256
    gather_forward(norm_parts[0], 0, *started[0], norm_fsend, norm_frecv)
    loads[0].wait()
    gather_end(started[0][1])
    for which in (1, 0, 2):
        for t in range(0, cols, step):
            at = slice(t, t + step)
            products[which, :, at] = dot(normed[0].reshape(rows, half), wqkv[which, :half, at])
    gather_forward(norm_parts[1], 1, *started[1], norm_fsend, norm_frecv)
    gather_end(started[1][1])

    def plane(k):
        return (band + k) % ns if spread_heads else 0

    def project(which, out):
        for t in range(cols // step):
            tile_at = slice(t * step, (t + 1) * step)
            p = dot(normed[1].reshape(rows, half), wqkv[which, half:, tile_at])
            p = (products[which, :, tile_at] + p).astype(BF16)
            span = min(step, gcols)
            for c in range(0, step, span):
                at = t * step + c
                out[at // gcols, :, at % gcols : at % gcols + span] = p[:, c : c + span]

    def to_bands(own, landing, ssem, rsem):
        return [
            send(own.at[plane(k)], landing.at[k - 1], ssem.at[k - 1], rsem.at[k - 1], seq=(band + k) % ns)
            for k in range(1, ns)
        ]

    project(1, keys_own)
    copies = to_bands(keys_own, keys_in, key_send, key_recv)
    project(0, query_own)
    if spread_heads:
        copies += to_bands(query_own, query_in, query_send, query_recv)
    project(2, values_own)
    value_copies = to_bands(values_own, values_in, value_send, value_recv)
    for copy in copies:
        copy.wait_recv()

    def all_rows(own, landing, at):
        return jnp.concatenate([own[plane(0), :, at]] + [landing[k, :, at] for k in range(ns - 1)], axis=0)

    sources = list(range(1, ns)) + [0] if spread_heads else [0]
    ready = {}
    for h in range(gcols // HD):
        at = slice(h * HD, (h + 1) * HD)
        keys = all_rows(keys_own, keys_in, at)
        for k in sources:
            q = query_in[k - 1, :, at] if k else query_own[plane(0), :, at]
            s = dot(q, keys, ((1,), (1,))) / math.sqrt(HD)
            e = jnp.exp(s - jnp.max(s, axis=-1, keepdims=True))
            ready[h, k] = e.astype(BF16), jnp.sum(e, axis=-1, keepdims=True)
    for copy in value_copies:
        copy.wait_recv()
    copies = []
    for k in sources:
        for h in range(gcols // HD):
            at = slice(h * HD, (h + 1) * HD)
            probs, total = ready[h, k]
            out = (dot(probs, all_rows(values_own, values_in, at)) / total).astype(BF16)
            if k:
                mixed[k - 1, :, at] = out
            else:
                attended[plane(0), :, at] = out
        if k:
            copies.append(
                send(
                    mixed.at[k - 1], attended.at[band], mixed_send.at[k - 1], mixed_recv.at[k - 1],
                    seq=(band + ns - k) % ns,
                )
            )
    for copy in copies:
        copy.wait_recv()

    loads[1].wait()
    attended_all = jnp.concatenate([attended[g] for g in range(groups)], axis=1)

    pairs = []
    for a in range(2):
        for b in range(ns):
            at = b * piece + a * sub
            p = dot(attended_all, wo[:, at : at + sub])
            for d in range(nv):
                part[a, d % 2, d // 2, :, b * sub : (b + 1) * sub] = p[d * share : (d + 1) * share]
        pairs.append(send(part.at[a, 1 - core], pair_in2.at[a], pair2_send.at[a], pair2_recv.at[a], var=mate))
    chips = [[], []]
    for a in range(2):
        pairs[a].wait_recv()
        for k in range(1, nch):
            j = chip_at(k)
            pair_sum2[a, k - 1] = (part[a, core, j] + pair_in2[a, j]).astype(BF16)
            at = a * (nch - 1) + k - 1
            chips[a].append(
                send(
                    pair_sum2.at[a, k - 1], chip_in2.at[a, k - 1], chip2_send.at[at], chip2_recv.at[at],
                    var=2 * j + core,
                )
            )

    copies = [[], []]
    for a in range(2):
        sums = agg[a].astype(F32) + (part[a, core, chip] + pair_in2[a, chip])
        for k in range(1, nch):
            chips[a][k - 1].wait_recv()
            sums = sums + chip_in2[a, k - 1].astype(F32)
        sums = sums.astype(BF16)
        for b in range(ns):
            layer[a, b] = sums[:, b * sub : (b + 1) * sub]
        for k in range(1, ns):
            to, at = (band + k) % ns, a * (ns - 1) + k - 1
            copies[a].append(
                send(layer.at[a, to], gathered.at[a, band, me], layer_send.at[at], layer_recv.at[at], seq=to)
            )
        gathered[a, band, me] = layer[a, band]
    last_parts = [lambda d, a=a: gathered.at[a, :, d] for a in range(2)]
    started = []
    for a in range(2):
        for copy in copies[a]:
            copy.wait_recv()
        started.append(gather_start(last_parts[a], a, last_send, last_recv, last_fsend, last_frecv))
    for a in range(2):
        gather_forward(last_parts[a], a, *started[a], last_fsend, last_frecv)
    for a in range(2):
        gather_end(started[a][1])
    for copy in cots:
        copy.wait_recv()
    for copy in pending:
        copy.wait_send()


def body(nv, ns, patches, patch_weight, var_embed, agg_query, norm_gain, qkv_weight, out_weight, head_cot):
    count, rows, pixels = patches.shape
    width = patch_weight.shape[2]
    heads = agg_query.shape[1]
    cols = out_weight.shape[0]
    share = rows // nv
    nch = nv // 2
    piece = width // ns
    groups = ns if cols // HD % ns == 0 else 1
    plane = (groups, rows, cols // groups)
    landing = (ns - 1, rows, cols // groups)
    dma = pltpu.SemaphoreType.DMA
    vmem = pl.BlockSpec(memory_space=pltpu.VMEM)
    anywhere = pl.BlockSpec(memory_space=pl.ANY)
    V = pltpu.VMEM
    gathered, cot_all = pl.pallas_call(
        functools.partial(kernel, nv, ns),
        out_shape=[
            jax.ShapeDtypeStruct((2, ns, nv, share, piece // 2), BF16),
            jax.ShapeDtypeStruct((ns,) + head_cot.shape, BF16),
        ],
        in_specs=[vmem, anywhere, vmem, vmem, vmem, anywhere, anywhere, vmem],
        out_specs=[vmem, vmem],
        scratch_shapes=[
            V((count, pixels, width), BF16),
            V((3, width, cols), BF16),
            V((cols, width), BF16),
            V((count, nv, share, width), BF16),
            V((count, nv, share, heads), F32),
            V((2, heads, rows), F32),
            V((nv - 1, 2, heads, rows), F32),
            V((nch, share, width), F32),
            V((2, nv, share, heads), F32),
            V((nch, share, width), F32),
            V((nch, share, width), F32),
            V((nch - 1, share, width), F32),
            V((2, share, width // 2), BF16),
            V((2, nv, share, width // 2), BF16),
            V(plane, BF16),
            V(plane, BF16),
            V(plane, BF16),
            V(landing, BF16),
            V(landing, BF16),
            V(landing, BF16),
            V(landing, BF16),
            V(plane, BF16),
            V((3, rows, cols), F32),
            V((2, 2, nch, share, width // 2), F32),
            V((2, nch, share, width // 2), F32),
            V((2, nch - 1, share, width // 2), BF16),
            V((2, nch - 1, share, width // 2), BF16),
            V((2, ns, share, piece // 2), BF16),
            dma((count,)), dma((2,)),
            dma((ns - 1,)), dma((ns - 1,)),
            dma((nv - 1,)), dma((nv - 1,)),
            dma((nch,)), dma((nch,)),
            dma((nch - 1,)), dma((nch - 1,)),
            dma((2 * nch - 2,)), dma((2 * nch - 2,)), dma((2 * nch,)), dma((2 * nch,)),
            dma((ns - 1,)), dma((ns - 1,)), dma((ns - 1,)), dma((ns - 1,)),
            dma((ns - 1,)), dma((ns - 1,)), dma((ns - 1,)), dma((ns - 1,)),
            dma((2,)), dma((2,)),
            dma((2 * nch - 2,)), dma((2 * nch - 2,)),
            dma((2 * ns - 2,)), dma((2 * ns - 2,)),
            dma((2 * nch - 2,)), dma((2 * nch - 2,)), dma((2 * nch,)), dma((2 * nch,)),
        ],
        compiler_params=pltpu.CompilerParams(
            collective_id=0, has_side_effects=True, vmem_limit_bytes=56 * 1024 * 1024
        ),
    )(
        jnp.transpose(patches, (0, 2, 1)),
        patch_weight,
        var_embed,
        jnp.transpose(agg_query),
        norm_gain,
        jnp.transpose(qkv_weight, (1, 0, 2)),
        out_weight,
        head_cot,
    )
    tokens = ns * rows
    grads = lax.dot_general(
        gathered.reshape(2, tokens, piece // 2),
        cot_all.reshape(tokens, head_cot.shape[1]),
        (((1,), (0,)), ((), ())),
        preferred_element_type=F32,
    )
    return grads.reshape(piece, head_cot.shape[1])


def solution(mesh):
    nv, ns = mesh.shape["var"], mesh.shape["seq"]
    return jax.shard_map(
        functools.partial(body, nv, ns),
        mesh=mesh,
        in_specs=(
            P("var", "seq", None),
            P("var", None, None),
            P("var", None),
            P(),
            P(),
            P(None, None, "var"),
            P("var", None),
            P("seq", "var"),
        ),
        out_specs=P("seq", "var"),
        check_vma=False,
    )
```

```python
import functools

import jax
import jax.numpy as jnp
from jax import lax
from jax.experimental import pallas as pl
from jax.experimental.pallas import tpu as pltpu
from jax.sharding import PartitionSpec as P

MESH = pl.DeviceIdType.MESH
F32 = jnp.float32
BF16 = jnp.bfloat16
eps = 1e-05
HD = 128


def dot(a, b, contract=((1,), (0,))):
    return lax.dot_general(a, b, (contract, ((), ())), preferred_element_type=F32)


def kernel(
    nv, ns,
    patches, pw_hbm, var_embed, query_map, gain, wqkv_hbm, wo_hbm, cot,
    gathered, cot_all,
    pw, wqkv, wo, emb, weights, stats_own, stats_in, for_mate, factor, pair_in, pair_sum, chip_in,
    agg, normed, keys_own, values_own, query_own, keys_in, values_in, query_in, mixed, attended, products,
    part, pair_in2, pair_sum2, chip_in2, layer,
    pw_sem, local_sem, cot_send, cot_recv, stats_send, stats_recv, pair_send, pair_recv, chip_send, chip_recv,
    norm_send, norm_recv, norm_fsend, norm_frecv, key_send, key_recv, value_send, value_recv,
    query_send, query_recv, mixed_send, mixed_recv,
    pair2_send, pair2_recv, chip2_send, chip2_recv, layer_send, layer_recv,
    last_send, last_recv, last_fsend, last_frecv,
):
    count, _, rows = patches.shape
    width = pw.shape[2]
    heads = width // HD
    nch = nv // 2
    share = rows // nv
    cols = wo.shape[0]
    piece = width // ns
    half = width // 2
    sub = piece // 2
    spread_heads = cols // HD % ns == 0
    groups, _, gcols = attended.shape
    me = lax.axis_index("var")
    band = lax.axis_index("seq")
    chip = me // 2
    core = me % 2
    mate = chip * 2 + (1 - core)
    order = sorted(range(1, nch), key=lambda k: -bin(k).count("1")) + [0]
    pending = []

    def chip_at(k):
        at, place = 0, 1
        while place < nch:
            bit = chip // place % 2
            at = at + place * (1 - bit if k // place % 2 else bit)
            place *= 2
        return at

    def settle(upto):
        for copy in pending[:upto]:
            copy.wait_send()
        del pending[:upto]

    def send(src, dst, ssem, rsem, **target):
        copy = pltpu.make_async_remote_copy(
            src_ref=src, dst_ref=dst, send_sem=ssem, recv_sem=rsem, device_id=target, device_id_type=MESH
        )
        copy.start()
        pending.append(copy)
        return copy

    embed_loads = [pltpu.make_async_copy(pw_hbm.at[v], pw.at[v], pw_sem.at[v]) for v in range(count)]
    for load in embed_loads:
        load.start()
    loads = [
        pltpu.make_async_copy(wqkv_hbm, wqkv, local_sem.at[0]),
        pltpu.make_async_copy(wo_hbm, wo, local_sem.at[1]),
    ]

    barrier = pltpu.get_barrier_semaphore()
    for k in range(1, nv):
        pl.semaphore_signal(barrier, inc=1, device_id={"var": (me + k) % nv}, device_id_type=MESH)
    for k in range(1, ns):
        pl.semaphore_signal(barrier, inc=1, device_id={"seq": (band + k) % ns}, device_id_type=MESH)

    tile = 512
    scores = []
    for v in range(count):
        embed_loads[v].wait()
        if v == count - 1:
            for load in loads:
                load.start()
        pixels = jnp.transpose(patches[v])
        s = None
        for t in range(0, width, tile):
            at = slice(t, t + tile)
            e = (dot(pixels, pw[v, :, at]) + var_embed[v : v + 1, at].astype(F32)).astype(BF16)
            for d in range(nv):
                emb[v, d, :, at] = e[d * share : (d + 1) * share]
            p = dot(e, query_map[:, at], ((1,), (1,)))
            s = p if s is None else s + p
        scores.append(s * HD**-0.5)
    peak = functools.reduce(jnp.maximum, scores)
    unscaled = [jnp.exp(s - peak) for s in scores]
    total = functools.reduce(jnp.add, unscaled)
    stats_own[0] = jnp.transpose(peak)
    stats_own[1] = jnp.transpose(total)

    pl.semaphore_wait(barrier, nv - 1 + ns - 1)
    stats = [
        send(stats_own, stats_in.at[k - 1], stats_send.at[k - 1], stats_recv.at[k - 1], var=(me + k) % nv)
        for k in range(1, nv)
    ]
    cots = [
        send(cot, cot_all.at[band], cot_send.at[k - 1], cot_recv.at[k - 1], seq=(band + k) % ns)
        for k in range(1, ns)
    ]
    cot_all[band] = cot[...]

    for v in range(count):
        w = unscaled[v]
        for d in range(nv):
            weights[v, d] = w[d * share : (d + 1) * share]

    def weighted(d):
        w = [weights[v, d] for v in range(count)]
        for h in range(heads):
            at = slice(h * HD, (h + 1) * HD)
            acc = w[0][:, h : h + 1] * emb[0, d, :, at].astype(F32)
            for v in range(1, count):
                acc = acc + w[v][:, h : h + 1] * emb[v, d, :, at].astype(F32)
            yield h, at, acc

    pairs = []
    for i, k in enumerate(order):
        for h, at, acc in weighted(2 * chip_at(k) + 1 - core):
            for_mate[i, :, at] = acc
        pairs.append(send(for_mate.at[i], pair_in.at[i], pair_send.at[i], pair_recv.at[i], var=mate))

    for copy in stats:
        copy.wait_recv()
    own_peak = stats_own[0]
    top = own_peak
    for k in range(nv - 1):
        top = jnp.maximum(top, stats_in[k, 0])
    whole = stats_own[1] * jnp.exp(own_peak - top)
    for k in range(nv - 1):
        whole = whole + stats_in[k, 1] * jnp.exp(stats_in[k, 0] - top)
    mate_peak = stats_in[(1 - core) * (nv - 2), 0]
    for which, part_peak in enumerate((own_peak, mate_peak)):
        scale = jnp.transpose(jnp.exp(part_peak - top) / whole)
        for d in range(nv):
            factor[which, d] = scale[d * share : (d + 1) * share]

    chips = []
    for i, k in enumerate(order):
        d = 2 * chip_at(k) + core
        own_factor, mate_factor = factor[0, d], factor[1, d]
        pairs[i].wait_recv()
        for h, at, acc in weighted(d):
            pair_sum[i, :, at] = acc * own_factor[:, h : h + 1] + pair_in[i, :, at] * mate_factor[:, h : h + 1]
        if k:
            chips.append(send(pair_sum.at[i], chip_in.at[i], chip_send.at[i], chip_recv.at[i], var=d))
    settle(len(stats) + len(cots) + len(pairs))
    for copy in chips:
        copy.wait_recv()
    sums = pair_sum[nch - 1]
    for i in range(nch - 1):
        sums = sums + chip_in[i]
    own = sums.astype(BF16)
    for a in range(2):
        for b in range(ns):
            agg[a, :, b * sub : (b + 1) * sub] = own[:, b * piece + a * sub : b * piece + (a + 1) * sub]

    own = own.astype(F32)
    center = jnp.mean(own, axis=-1, keepdims=True)
    shifted = own - center
    spread = jnp.mean(shifted * shifted, axis=-1, keepdims=True)
    own = (shifted * lax.rsqrt(spread + eps) * gain[...].astype(F32)[None, :]).astype(BF16)
    for a in range(2):
        normed[a, me] = own[:, a * half : (a + 1) * half]

    def gather_start(part_of, a, ssem, rsem, fsend, frecv):
        mine = part_of(me)
        at = a * (nch - 1) - 1
        direct = [
            send(mine, mine, ssem.at[at + k], rsem.at[at + k], var=2 * chip_at(k) + core) for k in range(1, nch)
        ]
        return direct, [send(mine, mine, fsend.at[a * nch], frecv.at[a * nch], var=mate)]

    def gather_forward(part_of, a, direct, across, fsend, frecv):
        for k in range(1, nch):
            direct[k - 1].wait_recv()
            got = part_of(2 * chip_at(k) + core)
            across.append(send(got, got, fsend.at[a * nch + k], frecv.at[a * nch + k], var=mate))

    def gather_end(across):
        for copy in across:
            copy.wait_recv()

    norm_parts = [lambda d, a=a: normed.at[a, d] for a in range(2)]
    started = [
        gather_start(norm_parts[a], a, norm_send, norm_recv, norm_fsend, norm_frecv) for a in range(2)
    ]

    step = 256
    gather_forward(norm_parts[0], 0, *started[0], norm_fsend, norm_frecv)
    loads[0].wait()
    gather_end(started[0][1])
    for which in (1, 0, 2):
        for t in range(0, cols, step):
            at = slice(t, t + step)
            products[which, :, at] = dot(normed[0].reshape(rows, half), wqkv[which, :half, at])
    gather_forward(norm_parts[1], 1, *started[1], norm_fsend, norm_frecv)
    gather_end(started[1][1])

    def plane(k):
        return (band + k) % ns if spread_heads else 0

    def project(which, out):
        for t in range(cols // step):
            tile_at = slice(t * step, (t + 1) * step)
            p = dot(normed[1].reshape(rows, half), wqkv[which, half:, tile_at])
            p = (products[which, :, tile_at] + p).astype(BF16)
            span = min(step, gcols)
            for c in range(0, step, span):
                at = t * step + c
                out[at // gcols, :, at % gcols : at % gcols + span] = p[:, c : c + span]

    def to_bands(own, landing, ssem, rsem):
        return [
            send(own.at[plane(k)], landing.at[k - 1], ssem.at[k - 1], rsem.at[k - 1], seq=(band + k) % ns)
            for k in range(1, ns)
        ]

    before = len(pending)
    project(1, keys_own)
    copies = to_bands(keys_own, keys_in, key_send, key_recv)
    project(0, query_own)
    if spread_heads:
        copies += to_bands(query_own, query_in, query_send, query_recv)
    project(2, values_own)
    value_copies = to_bands(values_own, values_in, value_send, value_recv)
    settle(before)
    for copy in copies:
        copy.wait_recv()

    def all_rows(own, landing, at):
        return jnp.concatenate([own[plane(0), :, at]] + [landing[k, :, at] for k in range(ns - 1)], axis=0)

    sources = list(range(1, ns)) + [0] if spread_heads else [0]
    ready = {}
    for h in range(gcols // HD):
        at = slice(h * HD, (h + 1) * HD)
        keys = all_rows(keys_own, keys_in, at)
        for k in sources:
            q = query_in[k - 1, :, at] if k else query_own[plane(0), :, at]
            s = dot(q, keys, ((1,), (1,))) * HD**-0.5
            e = jnp.exp(s - jnp.max(s, axis=-1, keepdims=True))
            ready[h, k] = e.astype(BF16), jnp.sum(e, axis=-1, keepdims=True)
    for copy in value_copies:
        copy.wait_recv()
    copies = []
    for k in sources:
        for h in range(gcols // HD):
            at = slice(h * HD, (h + 1) * HD)
            probs, total = ready[h, k]
            out = (dot(probs, all_rows(values_own, values_in, at)) / total).astype(BF16)
            if k:
                mixed[k - 1, :, at] = out
            else:
                attended[plane(0), :, at] = out
        if k:
            copies.append(
                send(
                    mixed.at[k - 1], attended.at[band], mixed_send.at[k - 1], mixed_recv.at[k - 1],
                    seq=(band + ns - k) % ns,
                )
            )
    for copy in copies:
        copy.wait_recv()

    loads[1].wait()
    attended_all = jnp.concatenate([attended[g] for g in range(groups)], axis=1)

    before = len(pending)
    pairs = []
    for a in range(2):
        for b in range(ns):
            at = b * piece + a * sub
            p = dot(attended_all, wo[:, at : at + sub])
            for d in range(nv):
                part[a, d % 2, d // 2, :, b * sub : (b + 1) * sub] = p[d * share : (d + 1) * share]
        pairs.append(send(part.at[a, 1 - core], pair_in2.at[a], pair2_send.at[a], pair2_recv.at[a], var=mate))
    chips = [[], []]
    for a in range(2):
        pairs[a].wait_recv()
        for k in range(1, nch):
            j = chip_at(k)
            pair_sum2[a, k - 1] = (part[a, core, j] + pair_in2[a, j]).astype(BF16)
            at = a * (nch - 1) + k - 1
            chips[a].append(
                send(
                    pair_sum2.at[a, k - 1], chip_in2.at[a, k - 1], chip2_send.at[at], chip2_recv.at[at],
                    var=2 * j + core,
                )
            )

    copies = [[], []]
    for a in range(2):
        sums = agg[a].astype(F32) + (part[a, core, chip] + pair_in2[a, chip])
        for k in range(1, nch):
            chips[a][k - 1].wait_recv()
            sums = sums + chip_in2[a, k - 1].astype(F32)
        sums = sums.astype(BF16)
        for b in range(ns):
            layer[a, b] = sums[:, b * sub : (b + 1) * sub]
        for k in range(1, ns):
            to, at = (band + k) % ns, a * (ns - 1) + k - 1
            copies[a].append(
                send(layer.at[a, to], gathered.at[band, me, :, a * sub : (a + 1) * sub], layer_send.at[at], layer_recv.at[at], seq=to)
            )
        gathered[band, me, :, a * sub : (a + 1) * sub] = layer[a, band]
    settle(before)
    last_parts = [lambda d, a=a: gathered.at[:, d, :, a * sub : (a + 1) * sub] for a in range(2)]
    started = []
    for a in range(2):
        for copy in copies[a]:
            copy.wait_recv()
        started.append(gather_start(last_parts[a], a, last_send, last_recv, last_fsend, last_frecv))
    for a in range(2):
        gather_forward(last_parts[a], a, *started[a], last_fsend, last_frecv)
    settle(len(pending) - 2 * (2 * nch - 1))
    for a in range(2):
        gather_end(started[a][1])
    for copy in cots:
        copy.wait_recv()
    settle(len(pending))


def body(nv, ns, patches, patch_weight, var_embed, agg_query, norm_gain, qkv_weight, out_weight, head_cot):
    count, rows, pixels = patches.shape
    width = patch_weight.shape[2]
    heads = agg_query.shape[1]
    cols = out_weight.shape[0]
    share = rows // nv
    nch = nv // 2
    piece = width // ns
    groups = ns if cols // HD % ns == 0 else 1
    plane = (groups, rows, cols // groups)
    landing = (ns - 1, rows, cols // groups)
    dma = pltpu.SemaphoreType.DMA
    vmem = pl.BlockSpec(memory_space=pltpu.VMEM)
    anywhere = pl.BlockSpec(memory_space=pl.ANY)
    V = pltpu.VMEM
    gathered, cot_all = pl.pallas_call(
        functools.partial(kernel, nv, ns),
        out_shape=[
            jax.ShapeDtypeStruct((ns, nv, share, piece), BF16),
            jax.ShapeDtypeStruct((ns,) + head_cot.shape, BF16),
        ],
        in_specs=[vmem, anywhere, vmem, vmem, vmem, anywhere, anywhere, vmem],
        out_specs=[vmem, vmem],
        scratch_shapes=[
            V((count, pixels, width), BF16),
            V((3, width, cols), BF16),
            V((cols, width), BF16),
            V((count, nv, share, width), BF16),
            V((count, nv, share, heads), F32),
            V((2, heads, rows), F32),
            V((nv - 1, 2, heads, rows), F32),
            V((nch, share, width), F32),
            V((2, nv, share, heads), F32),
            V((nch, share, width), F32),
            V((nch, share, width), F32),
            V((nch - 1, share, width), F32),
            V((2, share, width // 2), BF16),
            V((2, nv, share, width // 2), BF16),
            V(plane, BF16),
            V(plane, BF16),
            V(plane, BF16),
            V(landing, BF16),
            V(landing, BF16),
            V(landing, BF16),
            V(landing, BF16),
            V(plane, BF16),
            V((3, rows, cols), F32),
            V((2, 2, nch, share, width // 2), F32),
            V((2, nch, share, width // 2), F32),
            V((2, nch - 1, share, width // 2), BF16),
            V((2, nch - 1, share, width // 2), BF16),
            V((2, ns, share, piece // 2), BF16),
            dma((count,)), dma((2,)),
            dma((ns - 1,)), dma((ns - 1,)),
            dma((nv - 1,)), dma((nv - 1,)),
            dma((nch,)), dma((nch,)),
            dma((nch - 1,)), dma((nch - 1,)),
            dma((2 * nch - 2,)), dma((2 * nch - 2,)), dma((2 * nch,)), dma((2 * nch,)),
            dma((ns - 1,)), dma((ns - 1,)), dma((ns - 1,)), dma((ns - 1,)),
            dma((ns - 1,)), dma((ns - 1,)), dma((ns - 1,)), dma((ns - 1,)),
            dma((2,)), dma((2,)),
            dma((2 * nch - 2,)), dma((2 * nch - 2,)),
            dma((2 * ns - 2,)), dma((2 * ns - 2,)),
            dma((2 * nch - 2,)), dma((2 * nch - 2,)), dma((2 * nch,)), dma((2 * nch,)),
        ],
        compiler_params=pltpu.CompilerParams(
            collective_id=0, has_side_effects=True, vmem_limit_bytes=56 * 1024 * 1024
        ),
    )(
        jnp.transpose(patches, (0, 2, 1)),
        patch_weight,
        var_embed,
        jnp.transpose(agg_query),
        norm_gain,
        jnp.transpose(qkv_weight, (1, 0, 2)),
        out_weight,
        head_cot,
    )
    tokens = ns * rows
    return lax.dot_general(
        gathered.reshape(tokens, piece),
        cot_all.reshape(tokens, head_cot.shape[1]),
        (((0,), (0,)), ((), ())),
        preferred_element_type=F32,
    )


def solution(mesh):
    nv, ns = mesh.shape["var"], mesh.shape["seq"]
    return jax.shard_map(
        functools.partial(body, nv, ns),
        mesh=mesh,
        in_specs=(
            P("var", "seq", None),
            P("var", None, None),
            P("var", None),
            P(),
            P(),
            P(None, None, "var"),
            P("var", None),
            P("seq", "var"),
        ),
        out_specs=P("seq", "var"),
        check_vma=False,
    )
```

```python
import functools

import jax
import jax.numpy as jnp
from jax import lax
from jax.experimental import pallas as pl
from jax.experimental.pallas import tpu as pltpu
from jax.sharding import PartitionSpec as P

MESH = pl.DeviceIdType.MESH
F32 = jnp.float32
BF16 = jnp.bfloat16
eps = 1e-05
HD = 128


def dot(a, b, contract=((1,), (0,))):
    return lax.dot_general(a, b, (contract, ((), ())), preferred_element_type=F32)


def kernel(
    nv, ns,
    patches, pw_hbm, var_embed, query_map, gain, wqkv_hbm, wo_hbm, cot,
    gathered, cot_all,
    pw, wqkv, wo, emb, weights, stats_own, stats_in, for_mate, factor, pair_in, pair_sum, chip_in,
    agg, normed, keys_own, values_own, query_own, keys_in, values_in, query_in, mixed, attended, products,
    part, pair_in2, pair_sum2, chip_in2, layer,
    pw_sem, local_sem, cot_send, cot_recv, stats_send, stats_recv, pair_send, pair_recv, chip_send, chip_recv,
    norm_send, norm_recv, norm_fsend, norm_frecv, key_send, key_recv, value_send, value_recv,
    query_send, query_recv, mixed_send, mixed_recv,
    pair2_send, pair2_recv, chip2_send, chip2_recv, layer_send, layer_recv,
    last_send, last_recv, last_fsend, last_frecv,
):
    count, _, rows = patches.shape
    width = pw.shape[2]
    heads = width // HD
    nch = nv // 2
    share = rows // nv
    cols = wo.shape[0]
    piece = width // ns
    half = width // 2
    sub = piece // 2
    spread_heads = cols // HD % ns == 0
    groups, _, gcols = attended.shape
    me = lax.axis_index("var")
    band = lax.axis_index("seq")
    chip = me // 2
    core = me % 2
    mate = chip * 2 + (1 - core)
    order = sorted(range(1, nch), key=lambda k: -bin(k).count("1")) + [0]
    pending = []

    def chip_at(k):
        at, place = 0, 1
        while place < nch:
            bit = chip // place % 2
            at = at + place * (1 - bit if k // place % 2 else bit)
            place *= 2
        return at

    def settle(upto):
        for copy in pending[:upto]:
            copy.wait_send()
        del pending[:upto]

    def send(src, dst, ssem, rsem, **target):
        copy = pltpu.make_async_remote_copy(
            src_ref=src, dst_ref=dst, send_sem=ssem, recv_sem=rsem, device_id=target, device_id_type=MESH
        )
        copy.start()
        pending.append(copy)
        return copy

    embed_loads = [pltpu.make_async_copy(pw_hbm.at[v], pw.at[v], pw_sem.at[v]) for v in range(count)]
    for load in embed_loads:
        load.start()
    loads = [
        pltpu.make_async_copy(wqkv_hbm, wqkv, local_sem.at[0]),
        pltpu.make_async_copy(wo_hbm, wo, local_sem.at[1]),
    ]

    barrier = pltpu.get_barrier_semaphore()
    for k in range(1, nv):
        pl.semaphore_signal(barrier, inc=1, device_id={"var": (me + k) % nv}, device_id_type=MESH)
    for k in range(1, ns):
        pl.semaphore_signal(barrier, inc=1, device_id={"seq": (band + k) % ns}, device_id_type=MESH)

    tile = 512
    scores = []
    for v in range(count):
        embed_loads[v].wait()
        if v == count - 1:
            for load in loads:
                load.start()
        pixels = jnp.transpose(patches[v])
        s = None
        for t in range(0, width, tile):
            at = slice(t, t + tile)
            e = (dot(pixels, pw[v, :, at]) + var_embed[v : v + 1, at].astype(F32)).astype(BF16)
            for d in range(nv):
                emb[v, d, :, at] = e[d * share : (d + 1) * share]
            p = dot(e, query_map[:, at], ((1,), (1,)))
            s = p if s is None else s + p
        scores.append(s * HD**-0.5)
    peak = functools.reduce(jnp.maximum, scores)
    unscaled = [jnp.exp(s - peak) for s in scores]
    total = functools.reduce(jnp.add, unscaled)
    stats_own[0] = jnp.transpose(peak)
    stats_own[1] = jnp.transpose(total)

    pl.semaphore_wait(barrier, nv - 1 + ns - 1)
    stats = [
        send(stats_own, stats_in.at[k - 1], stats_send.at[k - 1], stats_recv.at[k - 1], var=(me + k) % nv)
        for k in range(1, nv)
    ]
    cots = [
        send(cot, cot_all.at[band], cot_send.at[k - 1], cot_recv.at[k - 1], seq=(band + k) % ns)
        for k in range(1, ns)
    ]
    cot_all[band] = cot[...]

    for v in range(count):
        w = unscaled[v]
        for d in range(nv):
            weights[v, d] = w[d * share : (d + 1) * share]

    def weighted(d):
        w = [weights[v, d] for v in range(count)]
        for h in range(heads):
            at = slice(h * HD, (h + 1) * HD)
            acc = w[0][:, h : h + 1] * emb[0, d, :, at].astype(F32)
            for v in range(1, count):
                acc = acc + w[v][:, h : h + 1] * emb[v, d, :, at].astype(F32)
            yield h, at, acc

    pairs = []
    for i, k in enumerate(order):
        for h, at, acc in weighted(2 * chip_at(k) + 1 - core):
            for_mate[i, :, at] = acc
        pairs.append(send(for_mate.at[i], pair_in.at[i], pair_send.at[i], pair_recv.at[i], var=mate))

    for copy in stats:
        copy.wait_recv()
    own_peak = stats_own[0]
    top = own_peak
    for k in range(nv - 1):
        top = jnp.maximum(top, stats_in[k, 0])
    whole = stats_own[1] * jnp.exp(own_peak - top)
    for k in range(nv - 1):
        whole = whole + stats_in[k, 1] * jnp.exp(stats_in[k, 0] - top)
    mate_peak = stats_in[(1 - core) * (nv - 2), 0]
    for which, part_peak in enumerate((own_peak, mate_peak)):
        scale = jnp.transpose(jnp.exp(part_peak - top) / whole)
        for d in range(nv):
            factor[which, d] = scale[d * share : (d + 1) * share]

    chips = []
    cut = slice(0, half), slice(half, width)
    for i, k in enumerate(order):
        d = 2 * chip_at(k) + core
        own_factor, mate_factor = factor[0, d], factor[1, d]
        pairs[i].wait_recv()
        for h, at, acc in weighted(d):
            pair_sum[i, :, at] = acc * own_factor[:, h : h + 1] + pair_in[i, :, at] * mate_factor[:, h : h + 1]
        if nch != 4 and k:
            chips.append(send(pair_sum.at[i], chip_in.at[i], chip_send.at[i], chip_recv.at[i], var=d))
        elif k:
            for a, to in enumerate((1, 2)):
                if k & to:
                    slot = 0 if k == 3 else 1
                    chips.append(
                        send(
                            pair_sum.at[i, :, cut[a]], chip_in.at[slot, :, cut[a]],
                            chip_send.at[len(chips)], chip_recv.at[len(chips)], var=2 * chip_at(to) + core,
                        )
                    )
    settle(len(stats) + len(cots) + len(pairs))
    if nch == 4:
        for a, i in enumerate((2, 1)):
            chips[a].wait_recv()
            pair_sum[i, :, cut[a]] = pair_sum[i, :, cut[a]] + chip_in[0, :, cut[a]]
            chips.append(
                send(
                    pair_sum.at[i, :, cut[a]], chip_in.at[2, :, cut[a]],
                    chip_send.at[len(chips)], chip_recv.at[len(chips)], var=2 * chip_at(i) + core,
                )
            )
        for copy in chips[2:]:
            copy.wait_recv()
        sums = pair_sum[3] + chip_in[1] + chip_in[2]
    else:
        for copy in chips:
            copy.wait_recv()
        sums = pair_sum[nch - 1]
        for i in range(nch - 1):
            sums = sums + chip_in[i]
    own = sums.astype(BF16)
    for a in range(2):
        for b in range(ns):
            agg[a, :, b * sub : (b + 1) * sub] = own[:, b * piece + a * sub : b * piece + (a + 1) * sub]

    own = own.astype(F32)
    center = jnp.mean(own, axis=-1, keepdims=True)
    shifted = own - center
    spread = jnp.mean(shifted * shifted, axis=-1, keepdims=True)
    own = (shifted * lax.rsqrt(spread + eps) * gain[...].astype(F32)[None, :]).astype(BF16)
    for a in range(2):
        normed[a, me] = own[:, a * half : (a + 1) * half]

    def gather_start(part_of, a, ssem, rsem, fsend, frecv):
        mine = part_of(me)
        at = a * (nch - 1) - 1
        direct = [
            send(mine, mine, ssem.at[at + k], rsem.at[at + k], var=2 * chip_at(k) + core) for k in range(1, nch)
        ]
        return direct, [send(mine, mine, fsend.at[a * nch], frecv.at[a * nch], var=mate)]

    def gather_forward(part_of, a, direct, across, fsend, frecv):
        for k in range(1, nch):
            direct[k - 1].wait_recv()
            got = part_of(2 * chip_at(k) + core)
            across.append(send(got, got, fsend.at[a * nch + k], frecv.at[a * nch + k], var=mate))

    def gather_end(across):
        for copy in across:
            copy.wait_recv()

    norm_parts = [lambda d, a=a: normed.at[a, d] for a in range(2)]
    started = [
        gather_start(norm_parts[a], a, norm_send, norm_recv, norm_fsend, norm_frecv) for a in range(2)
    ]

    step = 256
    gather_forward(norm_parts[0], 0, *started[0], norm_fsend, norm_frecv)
    loads[0].wait()
    gather_end(started[0][1])
    for which in (1, 0, 2):
        for t in range(0, cols, step):
            at = slice(t, t + step)
            products[which, :, at] = dot(normed[0].reshape(rows, half), wqkv[which, :half, at])
    gather_forward(norm_parts[1], 1, *started[1], norm_fsend, norm_frecv)
    gather_end(started[1][1])

    def plane(k):
        return (band + k) % ns if spread_heads else 0

    def project(which, out):
        for t in range(cols // step):
            tile_at = slice(t * step, (t + 1) * step)
            p = dot(normed[1].reshape(rows, half), wqkv[which, half:, tile_at])
            p = (products[which, :, tile_at] + p).astype(BF16)
            span = min(step, gcols)
            for c in range(0, step, span):
                at = t * step + c
                out[at // gcols, :, at % gcols : at % gcols + span] = p[:, c : c + span]

    def to_bands(own, landing, ssem, rsem):
        return [
            send(own.at[plane(k)], landing.at[k - 1], ssem.at[k - 1], rsem.at[k - 1], seq=(band + k) % ns)
            for k in range(1, ns)
        ]

    before = len(pending)
    project(1, keys_own)
    copies = to_bands(keys_own, keys_in, key_send, key_recv)
    project(0, query_own)
    if spread_heads:
        copies += to_bands(query_own, query_in, query_send, query_recv)
    project(2, values_own)
    value_copies = to_bands(values_own, values_in, value_send, value_recv)
    settle(before)
    for copy in copies:
        copy.wait_recv()

    def all_rows(own, landing, at):
        return jnp.concatenate([own[plane(0), :, at]] + [landing[k, :, at] for k in range(ns - 1)], axis=0)

    sources = list(range(1, ns)) + [0] if spread_heads else [0]
    ready = {}
    for h in range(gcols // HD):
        at = slice(h * HD, (h + 1) * HD)
        keys = all_rows(keys_own, keys_in, at)
        for k in sources:
            q = query_in[k - 1, :, at] if k else query_own[plane(0), :, at]
            s = dot(q, keys, ((1,), (1,))) * HD**-0.5
            e = jnp.exp(s - jnp.max(s, axis=-1, keepdims=True))
            ready[h, k] = e.astype(BF16), jnp.sum(e, axis=-1, keepdims=True)
    for copy in value_copies:
        copy.wait_recv()
    copies = []
    for k in sources:
        for h in range(gcols // HD):
            at = slice(h * HD, (h + 1) * HD)
            probs, total = ready[h, k]
            out = (dot(probs, all_rows(values_own, values_in, at)) / total).astype(BF16)
            if k:
                mixed[k - 1, :, at] = out
            else:
                attended[plane(0), :, at] = out
        if k:
            copies.append(
                send(
                    mixed.at[k - 1], attended.at[band], mixed_send.at[k - 1], mixed_recv.at[k - 1],
                    seq=(band + ns - k) % ns,
                )
            )
    for copy in copies:
        copy.wait_recv()

    loads[1].wait()
    attended_all = jnp.concatenate([attended[g] for g in range(groups)], axis=1)

    before = len(pending)
    pairs = []
    for a in range(2):
        for b in range(ns):
            at = b * piece + a * sub
            p = dot(attended_all, wo[:, at : at + sub])
            for d in range(nv):
                part[a, d % 2, d // 2, :, b * sub : (b + 1) * sub] = p[d * share : (d + 1) * share]
        pairs.append(send(part.at[a, 1 - core], pair_in2.at[a], pair2_send.at[a], pair2_recv.at[a], var=mate))
    chips = [[], []]
    for a in range(2):
        pairs[a].wait_recv()
        for k in range(1, nch):
            j = chip_at(k)
            pair_sum2[a, k - 1] = (part[a, core, j] + pair_in2[a, j]).astype(BF16)
            at = a * (nch - 1) + k - 1
            chips[a].append(
                send(
                    pair_sum2.at[a, k - 1], chip_in2.at[a, k - 1], chip2_send.at[at], chip2_recv.at[at],
                    var=2 * j + core,
                )
            )

    copies = [[], []]
    for a in range(2):
        sums = agg[a].astype(F32) + (part[a, core, chip] + pair_in2[a, chip])
        for k in range(1, nch):
            chips[a][k - 1].wait_recv()
            sums = sums + chip_in2[a, k - 1].astype(F32)
        sums = sums.astype(BF16)
        for b in range(ns):
            layer[a, b] = sums[:, b * sub : (b + 1) * sub]
        for k in range(1, ns):
            to, at = (band + k) % ns, a * (ns - 1) + k - 1
            copies[a].append(
                send(layer.at[a, to], gathered.at[band, me, :, a * sub : (a + 1) * sub], layer_send.at[at], layer_recv.at[at], seq=to)
            )
        gathered[band, me, :, a * sub : (a + 1) * sub] = layer[a, band]
    settle(before)
    last_parts = [lambda d, a=a: gathered.at[:, d, :, a * sub : (a + 1) * sub] for a in range(2)]
    started = []
    for a in range(2):
        for copy in copies[a]:
            copy.wait_recv()
        started.append(gather_start(last_parts[a], a, last_send, last_recv, last_fsend, last_frecv))
    for a in range(2):
        gather_forward(last_parts[a], a, *started[a], last_fsend, last_frecv)
    settle(len(pending) - 2 * (2 * nch - 1))
    for a in range(2):
        gather_end(started[a][1])
    for copy in cots:
        copy.wait_recv()
    settle(len(pending))


def body(nv, ns, patches, patch_weight, var_embed, agg_query, norm_gain, qkv_weight, out_weight, head_cot):
    count, rows, pixels = patches.shape
    width = patch_weight.shape[2]
    heads = agg_query.shape[1]
    cols = out_weight.shape[0]
    share = rows // nv
    nch = nv // 2
    piece = width // ns
    groups = ns if cols // HD % ns == 0 else 1
    plane = (groups, rows, cols // groups)
    landing = (ns - 1, rows, cols // groups)
    dma = pltpu.SemaphoreType.DMA
    vmem = pl.BlockSpec(memory_space=pltpu.VMEM)
    anywhere = pl.BlockSpec(memory_space=pl.ANY)
    V = pltpu.VMEM
    gathered, cot_all = pl.pallas_call(
        functools.partial(kernel, nv, ns),
        out_shape=[
            jax.ShapeDtypeStruct((ns, nv, share, piece), BF16),
            jax.ShapeDtypeStruct((ns,) + head_cot.shape, BF16),
        ],
        in_specs=[vmem, anywhere, vmem, vmem, vmem, anywhere, anywhere, vmem],
        out_specs=[vmem, vmem],
        scratch_shapes=[
            V((count, pixels, width), BF16),
            V((3, width, cols), BF16),
            V((cols, width), BF16),
            V((count, nv, share, width), BF16),
            V((count, nv, share, heads), F32),
            V((2, heads, rows), F32),
            V((nv - 1, 2, heads, rows), F32),
            V((nch, share, width), F32),
            V((2, nv, share, heads), F32),
            V((nch, share, width), F32),
            V((nch, share, width), F32),
            V((nch - 1, share, width), F32),
            V((2, share, width // 2), BF16),
            V((2, nv, share, width // 2), BF16),
            V(plane, BF16),
            V(plane, BF16),
            V(plane, BF16),
            V(landing, BF16),
            V(landing, BF16),
            V(landing, BF16),
            V(landing, BF16),
            V(plane, BF16),
            V((3, rows, cols), F32),
            V((2, 2, nch, share, width // 2), F32),
            V((2, nch, share, width // 2), F32),
            V((2, nch - 1, share, width // 2), BF16),
            V((2, nch - 1, share, width // 2), BF16),
            V((2, ns, share, piece // 2), BF16),
            dma((count,)), dma((2,)),
            dma((ns - 1,)), dma((ns - 1,)),
            dma((nv - 1,)), dma((nv - 1,)),
            dma((nch,)), dma((nch,)),
            dma((2 * nch - 2,)), dma((2 * nch - 2,)),
            dma((2 * nch - 2,)), dma((2 * nch - 2,)), dma((2 * nch,)), dma((2 * nch,)),
            dma((ns - 1,)), dma((ns - 1,)), dma((ns - 1,)), dma((ns - 1,)),
            dma((ns - 1,)), dma((ns - 1,)), dma((ns - 1,)), dma((ns - 1,)),
            dma((2,)), dma((2,)),
            dma((2 * nch - 2,)), dma((2 * nch - 2,)),
            dma((2 * ns - 2,)), dma((2 * ns - 2,)),
            dma((2 * nch - 2,)), dma((2 * nch - 2,)), dma((2 * nch,)), dma((2 * nch,)),
        ],
        compiler_params=pltpu.CompilerParams(
            collective_id=0, has_side_effects=True, vmem_limit_bytes=56 * 1024 * 1024
        ),
    )(
        jnp.transpose(patches, (0, 2, 1)),
        patch_weight,
        var_embed,
        jnp.transpose(agg_query),
        norm_gain,
        jnp.transpose(qkv_weight, (1, 0, 2)),
        out_weight,
        head_cot,
    )
    tokens = ns * rows
    return lax.dot_general(
        gathered.reshape(tokens, piece),
        cot_all.reshape(tokens, head_cot.shape[1]),
        (((0,), (0,)), ((), ())),
        preferred_element_type=F32,
    )


def solution(mesh):
    nv, ns = mesh.shape["var"], mesh.shape["seq"]
    return jax.shard_map(
        functools.partial(body, nv, ns),
        mesh=mesh,
        in_specs=(
            P("var", "seq", None),
            P("var", None, None),
            P("var", None),
            P(),
            P(),
            P(None, None, "var"),
            P("var", None),
            P("seq", "var"),
        ),
        out_specs=P("seq", "var"),
        check_vma=False,
    )
```
